256 devices in a mesh: fsdp: 8 (over y_lo, x), rep: 32 (over y_hi, z, core).
Axes of the slice: x: 4, y: 4 (y_hi: 2, y_lo: 2; y = y_hi * 2 + y_lo), z: 8, core: 2. Of those that a mesh axis runs over, the one named last changes fastest.
Arguments:
- grads: bfloat16 [8, 32, 2, 512, 512], P('fsdp', 'rep'), may hold values from -0.25 to 0.25
- targets: int32 [8, 32, 2], P(None, 'rep'), may hold values from 0 to 15, as said below
- left_factor: float32 [8, 32, 2, 512, 512], P('fsdp', 'rep'), as said below
- right_factor: float32 [8, 32, 2, 512, 512], P('fsdp', 'rep'), as said below
- left_root: bfloat16 [8, 32, 2, 512, 512], P('fsdp', 'rep'), as said below
- right_root: bfloat16 [8, 32, 2, 512, 512], P('fsdp', 'rep'), as said below
- refresh: int32 [8, 32, 2], P('fsdp', 'rep'), may hold values 0 or 1
- buddy_offset: int32 [8], P('fsdp'), may hold values from 1 to 31
Outputs:
- new_left: bfloat16 [8, 32, 2, 512, 512], P('fsdp', 'rep')
- new_right: bfloat16 [8, 32, 2, 512, 512], P('fsdp', 'rep')
- buddy_left: bfloat16 [8, 32, 2, 512, 512], P('fsdp', 'rep')
- buddy_right: bfloat16 [8, 32, 2, 512, 512], P('fsdp', 'rep')
- precond: bfloat16 [8, 32, 2, 512, 512], P('fsdp', 'rep')
The draws below stay inside these ranges and needn't reach their ends.
Inputs may be any that keep to these rules, and one draw needn't show every extreme that they name: `targets`: for each replica index r, the blocks (f, r, k) fill every (owner, slot) pair exactly once; one device sends at most 1 block to one owner, and some device does so. `left_factor`: symmetric and positive definite. `right_factor`: symmetric and positive definite. `left_root`: symmetric. `right_root`: symmetric.
All inputs are finite; a program needn't handle non-finite values. No bound on the sum of `refresh` on one device may be relied on, other than what follows from the above.
Results may differ from the reference program's by a relative error of at most 0.0057.
Values may be sent and summed in bfloat16 or wider, within the bound.
No kernel may reach another device: no remote copies, remote signals or barrier semaphores. Data moves between devices by JAX's collectives and lax.ppermute only.
A program may use at most 128 MiB of HBM per device.

```python
import jax
import jax.numpy as jnp
from jax import lax

B = 512
BLK_DEV = 2
N_FSDP = 8
N_REP = 32


def factor_diagonal(key, lower, upper):
    share = jax.random.uniform(key, (N_FSDP, N_REP, BLK_DEV, B), jnp.float32)
    return lower * (upper / lower) ** share


def symmetric_noise(key, spread):
    raw = jax.random.uniform(key, (N_FSDP, N_REP, BLK_DEV, B, B), jnp.float32, -spread, spread)
    return 0.5 * (raw + jnp.swapaxes(raw, -1, -2))


def with_diagonal(noise, values):
    identity = jnp.eye(B, dtype=jnp.float32)
    return noise * (1.0 - identity) + values[..., :, None] * identity


def draw_left_factor(key, part):
    values = factor_diagonal(jax.random.fold_in(key, 11), 3.0, 8.0)
    key = jax.random.fold_in(key, 1)
    return with_diagonal(symmetric_noise(key, 2.4 / B ** 0.5), values)


def draw_left_root(key, part):
    values = factor_diagonal(jax.random.fold_in(key, 11), 3.0, 8.0)
    key = jax.random.fold_in(key, 2)
    return with_diagonal(symmetric_noise(key, 0.3 / B ** 0.5), values ** (-0.25)).astype(jnp.bfloat16)


def draw_right_factor(key, part):
    values = factor_diagonal(jax.random.fold_in(key, 12), 3.0, 8.0)
    key = jax.random.fold_in(key, 3)
    return with_diagonal(symmetric_noise(key, 2.4 / B ** 0.5), values)


def draw_right_root(key, part):
    values = factor_diagonal(jax.random.fold_in(key, 12), 3.0, 8.0)
    key = jax.random.fold_in(key, 4)
    return with_diagonal(symmetric_noise(key, 0.3 / B ** 0.5), values ** (-0.25)).astype(jnp.bfloat16)


def draw_targets(key, part):
    key = jax.random.fold_in(key, 5)
    key_perm, key_shift, key_slot = jax.random.split(key, 3)
    owner_perm = jax.vmap(lambda sub: jax.random.permutation(sub, N_FSDP))(jax.random.split(key_perm, N_REP))
    shifts = jax.random.randint(key_shift, (N_REP,), 0, N_FSDP)
    slot_perm = jax.vmap(lambda sub: jax.random.permutation(sub, BLK_DEV))(jax.random.split(key_slot, N_REP))
    blocks = jnp.arange(BLK_DEV, dtype=jnp.int32)
    owner = (jnp.transpose(owner_perm)[:, :, None] + blocks[None, None, :] + shifts[None, :, None]) % N_FSDP
    slots = jnp.broadcast_to(slot_perm[None, :, :], (N_FSDP, N_REP, BLK_DEV))
    return (owner * BLK_DEV + slots).astype(jnp.int32)


def with_ends(entries, own_key, low, largest):
    extent = entries.shape
    spot = [jax.random.randint(jax.random.fold_in(own_key, axis), (), 0, extent[axis]) for axis in range(len(extent))]
    entries = entries.at[tuple(spot)].set(low)
    longest = extent.index(max(extent))
    spot[longest] = (spot[longest] + 1) % extent[longest]
    return entries.at[tuple(spot)].set(largest)


def block_scale(rng, shape, cuts, least, largest):
    def one(dim, shards_of):
        steps = jax.random.uniform(jax.random.fold_in(jax.random.fold_in(rng, 6), dim), (shards_of,), jnp.float32, least / len(cuts), largest / len(cuts))
        return jnp.repeat(jnp.exp(steps), shape[dim] // shards_of).reshape((-1,) + (1,) * (len(shape) - dim - 1))

    loudness = one(*cuts[0])
    for cut in cuts[1:]:
        loudness = loudness * one(*cut)
    return loudness


def bell_draw(own_key, dims, deviation, most, pieces=(), kind=jnp.bfloat16):
    array = jax.random.normal(own_key, dims, jnp.float32) * deviation
    if len(pieces) > 0:
        array = block_scale(own_key, dims, pieces, -0.22, 0.18) * array
    return jnp.clip(array, min=-most, max=most).astype(kind)


def setup_inputs(seed: int = 0) -> dict:
    splits = jax.random.split(jax.random.key(seed), 9)
    grads = bell_draw(splits[0], (N_FSDP, N_REP, BLK_DEV, B, B), B ** -0.5, 0.25, ((0, 8), (1, 32)))
    targets = draw_targets(jax.random.fold_in(splits[8], 71), 0)
    left_factor = draw_left_factor(jax.random.fold_in(splits[8], 71), 0)
    right_factor = draw_right_factor(jax.random.fold_in(splits[8], 71), 0)
    left_root = draw_left_root(jax.random.fold_in(splits[8], 71), 0)
    right_root = draw_right_root(jax.random.fold_in(splits[8], 71), 0)
    refresh = with_ends((jax.random.randint(splits[6], (N_FSDP, N_REP, BLK_DEV), 0, 2) < 1).astype(jnp.int32), jax.random.fold_in(splits[6], 1), 0, 1)
    buddy_offset = with_ends(jax.random.randint(splits[7], (N_FSDP,), 1, N_REP), jax.random.fold_in(splits[7], 1), 1, N_REP - 1).astype(jnp.int32)
    return dict(grads=grads, targets=targets, left_factor=left_factor, right_factor=right_factor, left_root=left_root, right_root=right_root, refresh=refresh, buddy_offset=buddy_offset)


def newton(factor, root):
    high = lax.Precision.HIGHEST
    square = jnp.dot(root, root, precision=high)
    fourth = jnp.dot(square, square, precision=high)
    moment = jnp.dot(fourth, factor, precision=high)
    return (5.0 * root - jnp.dot(root, moment, precision=high)) / 4.0


def reference(grads, targets, left_factor, right_factor, left_root, right_root, refresh, buddy_offset):
    width = grads.shape[-1]
    per_dev = targets.shape[2]
    owner = targets // per_dev
    slot = targets % per_dev
    rep_ids = jnp.arange(N_REP, dtype=jnp.int32)[None, :, None]
    flat_slot = ((owner * N_REP + rep_ids) * per_dev + slot).astype(jnp.int32).reshape(-1)
    total = flat_slot.shape[0]
    source = jnp.zeros((total,), jnp.int32).at[flat_slot].set(jnp.arange(total, dtype=jnp.int32))
    grad_flat = grads.reshape(total, width, width)
    left_flat = left_factor.reshape(total, width, width)
    right_flat = right_factor.reshape(total, width, width)
    lroot_flat = left_root.reshape(total, width, width)
    rroot_flat = right_root.reshape(total, width, width)
    mask_flat = refresh.reshape(total)

    def one_slot(index):
        block = grad_flat[source[index]]
        lfac = left_flat[index] + jnp.dot(block, block.T, preferred_element_type=jnp.float32)
        rfac = right_flat[index] + jnp.dot(block.T, block, preferred_element_type=jnp.float32)
        lold = lroot_flat[index].astype(jnp.float32)
        rold = rroot_flat[index].astype(jnp.float32)
        flag = mask_flat[index] == 1
        lnew = jnp.where(flag, newton(lfac, lold), lold).astype(jnp.bfloat16)
        rnew = jnp.where(flag, newton(rfac, rold), rold).astype(jnp.bfloat16)
        half = jnp.dot(lnew, block, preferred_element_type=jnp.float32).astype(jnp.bfloat16)
        result = jnp.dot(half, rnew, preferred_element_type=jnp.float32).astype(jnp.bfloat16)
        return lnew, rnew, result

    lnew, rnew, result = lax.map(one_slot, jnp.arange(total, dtype=jnp.int32))
    shape = grads.shape
    new_left = lnew.reshape(shape)
    new_right = rnew.reshape(shape)
    precond = result[flat_slot].reshape(shape)
    partner = jnp.bitwise_xor(jnp.arange(N_REP, dtype=jnp.int32)[None, :], buddy_offset[:, None]).astype(jnp.int32)
    pick = partner[:, :, None, None, None]
    buddy_left = jnp.take_along_axis(new_left, pick, axis=1)
    buddy_right = jnp.take_along_axis(new_right, pick, axis=1)
    return new_left, new_right, buddy_left, buddy_right, precond
```

```python
import jax
import jax.numpy as jnp
from jax import lax
from jax.experimental import pallas as pl
from jax.experimental.pallas import tpu as pltpu
from jax.sharding import PartitionSpec as P

BF = jnp.bfloat16
F32 = jnp.float32
MIB = 2**20
PREP = 56
UPD = 56


def dot(a, b):
    return jnp.dot(a, b, preferred_element_type=F32)


def dot_nt(a, b):
    return lax.dot_general(a, b, (((1,), (1,)), ((), ())), preferred_element_type=F32)


def split(a):
    high = a.astype(BF)
    return high, (a - high.astype(F32)).astype(BF)


def dot3(a, b):
    return dot(a[0], b[0]) + (dot(a[0], b[1]) + dot(a[1], b[0]))


def cut_kernel(x_ref, o_ref, sems):
    copies = [
        pltpu.make_async_copy(x_ref.at[block], o_ref.at[:, block], sems.at[block])
        for block in range(x_ref.shape[0])
    ]
    for copy in copies:
        copy.start()
    for copy in copies:
        copy.wait()


def cut_blocks(blocks):
    per_dev, groups, rows, width = blocks.shape
    return pl.pallas_call(
        cut_kernel,
        out_shape=jax.ShapeDtypeStruct((groups, per_dev, rows, width), blocks.dtype),
        in_specs=[pl.BlockSpec(memory_space=pl.ANY)],
        out_specs=pl.BlockSpec(memory_space=pltpu.VMEM),
        scratch_shapes=[pltpu.SemaphoreType.DMA((per_dev,))],
        compiler_params=pltpu.CompilerParams(vmem_limit_bytes=PREP * MIB),
        name="cut_blocks",
    )(blocks)


def pick_kernel(order_ref, x_ref, o_ref, sems):
    copies = [
        pltpu.make_async_copy(x_ref.at[order_ref[slot]], o_ref.at[slot], sems.at[slot])
        for slot in range(o_ref.shape[0])
    ]
    for copy in copies:
        copy.start()
    for copy in copies:
        copy.wait()


def pick_pieces(order, pieces):
    count = order.shape[0]
    return pl.pallas_call(
        pick_kernel,
        out_shape=jax.ShapeDtypeStruct((count,) + pieces.shape[1:], pieces.dtype),
        in_specs=[
            pl.BlockSpec(memory_space=pltpu.SMEM),
            pl.BlockSpec(memory_space=pl.ANY),
        ],
        out_specs=pl.BlockSpec(memory_space=pl.ANY),
        scratch_shapes=[pltpu.SemaphoreType.DMA((count,))],
        compiler_params=pltpu.CompilerParams(vmem_limit_bytes=MIB),
        name="pick_pieces",
    )(order, pieces)


def choose_kernel(which_ref, slot_ref, *refs):
    arrays, o_ref, sems = refs[:-2], refs[-2], refs[-1]
    count = o_ref.shape[0]
    for block in range(count):
        for index, array in enumerate(arrays):

            @pl.when(which_ref[block] == index)
            def _():
                pltpu.make_async_copy(
                    array.at[slot_ref[block]], o_ref.at[block], sems.at[block]
                ).start()

    for block in range(count):
        pltpu.make_async_copy(arrays[0].at[0], o_ref.at[block], sems.at[block]).wait()


def choose_blocks(which, slot, arrays):
    shape = arrays[0].shape
    return pl.pallas_call(
        choose_kernel,
        out_shape=jax.ShapeDtypeStruct(shape, arrays[0].dtype),
        in_specs=[pl.BlockSpec(memory_space=pltpu.SMEM)] * 2
        + [pl.BlockSpec(memory_space=pl.ANY)] * len(arrays),
        out_specs=pl.BlockSpec(memory_space=pltpu.VMEM),
        scratch_shapes=[pltpu.SemaphoreType.DMA((shape[0],))],
        compiler_params=pltpu.CompilerParams(vmem_limit_bytes=4 * MIB),
        name="choose_blocks",
    )(which, slot, *arrays)


def prepare_kernel(flag_ref, f_ref, x_ref, high_ref, low_ref, rest_ref):
    @pl.when(flag_ref[pl.program_id(0)] == 1)
    def _():
        root = x_ref[0]
        square = split(dot(root, root))
        fourth = split(dot3(square, square))
        fifth = split(dot(root, fourth[0]) + dot(root, fourth[1]))
        high_ref[0] = fifth[0]
        low_ref[0] = fifth[1]
        rest_ref[0] = 5.0 * root.astype(F32) - dot3(fifth, split(f_ref[0]))


def prepare(flag, factor, root):
    per_dev, width, _ = root.shape
    whole = pl.BlockSpec((1, width, width), lambda s: (s, 0, 0))
    half = jax.ShapeDtypeStruct((per_dev, width, width), BF)
    full = jax.ShapeDtypeStruct((per_dev, width, width), F32)
    return pl.pallas_call(
        prepare_kernel,
        grid=(per_dev,),
        out_shape=(half, half, full),
        in_specs=[pl.BlockSpec(memory_space=pltpu.SMEM)] + [whole] * 2,
        out_specs=[whole] * 3,
        compiler_params=pltpu.CompilerParams(vmem_limit_bytes=PREP * MIB),
        cost_estimate=pl.CostEstimate(
            flops=9 * 2 * per_dev * width**3,
            bytes_accessed=14 * per_dev * width**2,
            transcendentals=0,
        ),
        name="prepare",
    )(flag, factor, root)


def finish_one(high, low, rest, first, second):
    part = split(first(high) + first(low))
    return (0.25 * (rest - (second(part[0]) + second(part[1])))).astype(BF)


def update_kernel(
    flag_ref, g_ref, lr_ref, rr_ref, lh, ll, lw, rh, rl, rw, ln_ref, rn_ref, res_ref
):
    width = lr_ref.shape[-1]
    own = g_ref[...].reshape(width, width)
    ln_ref[0] = lr_ref[0]
    rn_ref[0] = rr_ref[0]

    @pl.when(flag_ref[pl.program_id(0)] == 1)
    def _():
        right = lambda a: dot(a, own)
        across = lambda a: dot_nt(a, own)
        ln_ref[0] = finish_one(lh[0], ll[0], lw[0], right, across)
        rn_ref[0] = finish_one(rh[0], rl[0], rw[0], across, right)

    half = dot(ln_ref[0], own).astype(BF)
    res_ref[0] = dot(half, rn_ref[0]).astype(BF)


def update(flag, pieces, lroot, rroot, prepared):
    groups, per_dev, rows, width = pieces.shape
    whole = pl.BlockSpec((1, width, width), lambda s: (s, 0, 0))
    cut = pl.BlockSpec((groups, 1, rows, width), lambda s: (0, s, 0, 0))
    shape = jax.ShapeDtypeStruct((per_dev, width, width), BF)
    return pl.pallas_call(
        update_kernel,
        grid=(per_dev,),
        out_shape=(
            shape,
            shape,
            shape,
        ),
        in_specs=[pl.BlockSpec(memory_space=pltpu.SMEM), cut] + [whole] * 8,
        out_specs=(
            whole,
            whole,
            whole,
        ),
        compiler_params=pltpu.CompilerParams(vmem_limit_bytes=UPD * MIB),
        name="update",
    )(flag, pieces, lroot, rroot, *prepared)


def swap_cores(roots):
    pairs = [(source, source ^ 1) for source in range(lax.axis_size("rep"))]
    return lax.ppermute(roots, "rep", pairs)


def swap_owners(blocks, mask):
    pairs = [(source, source ^ mask) for source in range(lax.axis_size("fsdp"))]
    return lax.ppermute(blocks, "fsdp", pairs)


def swap_chips(offset, roots):
    size = lax.axis_size("rep")

    def branch(mask):
        pairs = [(source, source ^ mask) for source in range(size)]
        return lambda value: lax.ppermute(value, "rep", pairs)

    branches = [lambda value: value] + [branch(mask) for mask in range(2, size, 2)]
    return lax.switch(lax.shift_right_logical(offset, 1), branches, roots)


def exchange(pieces):
    return lax.all_to_all(pieces, "fsdp", 0, 0, tiled=True)


def per_device(
    grads, targets, left_factor, right_factor, left_root, right_root, refresh, buddy_offset
):
    groups = lax.axis_size("fsdp")
    shape = grads.shape
    per_dev, width = shape[2], shape[3]
    total = groups * per_dev
    rows = width // groups
    cut = (groups, per_dev, rows, width)
    flag = refresh[0, 0]
    flat = targets[:, 0, :].reshape(total)
    ids = jnp.arange(total, dtype=jnp.int32)
    source = jnp.sum(jnp.where(flat[None, :] == ids[:, None], ids[None, :], 0), axis=1)
    myself = lax.axis_index("fsdp")
    across = groups // 2
    table = targets[:, 0, :]
    mine = lax.dynamic_index_in_dim(table, myself, 0, keepdims=False)
    theirs = lax.dynamic_index_in_dim(table, myself ^ across, 0, keepdims=False)
    side = (mine // per_dev) ^ myself
    offset = buddy_offset[0]
    crossing = lax.rem(offset, 2) == 1

    spread = exchange(cut_blocks(grads.reshape(per_dev, groups, rows, width)))
    left = prepare(flag, left_factor[0, 0], left_root[0, 0])
    sorted_pieces = pick_pieces(source, spread.reshape(total, rows, width))
    sorted_pieces, left = lax.optimization_barrier((sorted_pieces, left))
    owned = exchange(sorted_pieces.reshape(cut))
    right = prepare(flag, right_factor[0, 0], right_root[0, 0])
    lnew, rnew, result = update(flag, owned, left_root[0, 0], right_root[0, 0], left + right)

    row = tuple(swap_owners(result, mask) for mask in range(1, across))
    rmoved = swap_cores(rnew)
    lfar = swap_chips(offset, lnew)
    row, rmoved, lfar = lax.optimization_barrier((row, rmoved, lfar))
    rnear = jnp.where(crossing, rmoved, rnew)
    row = (result,) + row
    leaving = choose_blocks(
        ((theirs // per_dev) ^ myself) % across, theirs % per_dev, row
    )
    other = swap_owners(leaving, across)
    lmoved = swap_cores(lfar)
    rcopy = swap_chips(offset, rnear)
    other, lmoved, rcopy = lax.optimization_barrier((other, lmoved, rcopy))
    lcopy = jnp.where(crossing, lmoved, lfar)
    precond = choose_blocks(
        jnp.minimum(side, across),
        jnp.where(side < across, mine % per_dev, jnp.arange(per_dev, dtype=jnp.int32)),
        row + (other,),
    )
    return (
        lnew.reshape(shape),
        rnew.reshape(shape),
        lcopy.reshape(shape),
        rcopy.reshape(shape),
        precond.reshape(shape),
    )


def solution(mesh):
    block = P("fsdp", "rep", None, None, None)
    placed = (
        block,
        P(None, "rep", None),
        block,
        block,
        block,
        block,
        P("fsdp", "rep", None),
        P("fsdp"),
    )
    return jax.shard_map(
        per_device,
        mesh=mesh,
        in_specs=placed,
        out_specs=(block,) * 5,
        check_vma=False,
    )
```

```python
import functools

import jax
import jax.numpy as jnp
from jax import lax
from jax.experimental import pallas as pl
from jax.experimental.pallas import tpu as pltpu
from jax.sharding import PartitionSpec as P

BF = jnp.bfloat16
F32 = jnp.float32
MIB = 2**20
PREP = 56
UPD = 56
CHOOSE = 8


def dot(a, b):
    return jnp.dot(a, b, preferred_element_type=F32)


def dot_nt(a, b):
    return lax.dot_general(a, b, (((1,), (1,)), ((), ())), preferred_element_type=F32)


def split(a):
    high = a.astype(BF)
    return high, (a - high.astype(F32)).astype(BF)


def dot3(a, b):
    return dot(a[0], b[0]) + (dot(a[0], b[1]) + dot(a[1], b[0]))


def cut_kernel(x_ref, o_ref, sems):
    copies = [
        pltpu.make_async_copy(x_ref.at[block], o_ref.at[:, block], sems.at[block])
        for block in range(x_ref.shape[0])
    ]
    for copy in copies:
        copy.start()
    for copy in copies:
        copy.wait()


def cut_blocks(blocks):
    per_dev, groups, rows, width = blocks.shape
    return pl.pallas_call(
        cut_kernel,
        out_shape=jax.ShapeDtypeStruct((groups, per_dev, rows, width), blocks.dtype),
        in_specs=[pl.BlockSpec(memory_space=pl.ANY)],
        out_specs=pl.BlockSpec(memory_space=pltpu.VMEM),
        scratch_shapes=[pltpu.SemaphoreType.DMA((per_dev,))],
        compiler_params=pltpu.CompilerParams(vmem_limit_bytes=PREP * MIB),
        name="cut_blocks",
    )(blocks)


def pick_kernel(order_ref, x_ref, o_ref, sems):
    copies = [
        pltpu.make_async_copy(x_ref.at[order_ref[slot]], o_ref.at[slot], sems.at[slot])
        for slot in range(o_ref.shape[0])
    ]
    for copy in copies:
        copy.start()
    for copy in copies:
        copy.wait()


def pick_pieces(order, pieces):
    count = order.shape[0]
    return pl.pallas_call(
        pick_kernel,
        out_shape=jax.ShapeDtypeStruct((count,) + pieces.shape[1:], pieces.dtype),
        in_specs=[
            pl.BlockSpec(memory_space=pltpu.SMEM),
            pl.BlockSpec(memory_space=pl.ANY),
        ],
        out_specs=pl.BlockSpec(memory_space=pl.ANY),
        scratch_shapes=[pltpu.SemaphoreType.DMA((count,))],
        compiler_params=pltpu.CompilerParams(vmem_limit_bytes=MIB),
        name="pick_pieces",
    )(order, pieces)


def choose_kernel(count, which_ref, slot_ref, *refs):
    arrays, outs = refs[:count], refs[count:-3]
    held, in_sems, out_sems = refs[-3:]
    per_out = outs[0].shape[0]
    total = held.shape[0]
    for block in range(total):
        for index, array in enumerate(arrays):

            @pl.when(which_ref[block] == index)
            def _():
                pltpu.make_async_copy(
                    array.at[slot_ref[block]], held.at[block], in_sems.at[block]
                ).start()

    leaving = [
        pltpu.make_async_copy(
            held.at[block],
            outs[block // per_out].at[block % per_out],
            out_sems.at[block],
        )
        for block in range(total)
    ]
    for block in range(total):
        pltpu.make_async_copy(arrays[0].at[0], held.at[block], in_sems.at[block]).wait()
        leaving[block].start()
    for copy in leaving:
        copy.wait()


def choose_blocks(which, slot, arrays):
    shape, dtype = arrays[0].shape, arrays[0].dtype
    total = which.shape[0]
    outs = total // shape[0]
    return pl.pallas_call(
        functools.partial(choose_kernel, len(arrays)),
        out_shape=(jax.ShapeDtypeStruct(shape, dtype),) * outs,
        in_specs=[pl.BlockSpec(memory_space=pltpu.SMEM)] * 2
        + [pl.BlockSpec(memory_space=pl.ANY)] * len(arrays),
        out_specs=(pl.BlockSpec(memory_space=pl.ANY),) * outs,
        scratch_shapes=[
            pltpu.VMEM((total,) + shape[1:], dtype),
            pltpu.SemaphoreType.DMA((total,)),
            pltpu.SemaphoreType.DMA((total,)),
        ],
        compiler_params=pltpu.CompilerParams(vmem_limit_bytes=CHOOSE * MIB),
        name="choose_blocks",
    )(which, slot, *arrays)


def prepare_kernel(flag_ref, f_ref, x_ref, pair_ref, rest_ref):
    width = x_ref.shape[-1]

    @pl.when(flag_ref[pl.program_id(0)] == 1)
    def _():
        root = x_ref[0]
        square = split(dot(root, root))
        fourth = split(dot3(square, square))
        fifth = split(dot(root, fourth[0]) + dot(root, fourth[1]))
        pair_ref[0, :, :width] = fifth[0]
        pair_ref[0, :, width:] = fifth[1]
        rest_ref[0] = 5.0 * root.astype(F32) - dot3(fifth, split(f_ref[0]))


def prepare(flag, factor, root):
    per_dev, width, _ = root.shape
    whole = pl.BlockSpec((1, width, width), lambda s: (s, 0, 0))
    wide = pl.BlockSpec((1, width, 2 * width), lambda s: (s, 0, 0))
    pair = jax.ShapeDtypeStruct((per_dev, width, 2 * width), BF)
    full = jax.ShapeDtypeStruct((per_dev, width, width), F32)
    return pl.pallas_call(
        prepare_kernel,
        grid=(per_dev,),
        out_shape=(pair, full),
        in_specs=[pl.BlockSpec(memory_space=pltpu.SMEM)] + [whole] * 2,
        out_specs=[wide, whole],
        compiler_params=pltpu.CompilerParams(vmem_limit_bytes=PREP * MIB),
        cost_estimate=pl.CostEstimate(
            flops=9 * 2 * per_dev * width**3,
            bytes_accessed=14 * per_dev * width**2,
            transcendentals=0,
        ),
        name="prepare",
    )(flag, factor, root)


def finish_one(pair, rest, first, second):
    width = rest.shape[-1]
    part = split(first(pair[:, :width]) + first(pair[:, width:]))
    return (0.25 * (rest - (second(part[0]) + second(part[1])))).astype(BF)


def update_kernel(
    flag_ref,
    g_ref,
    roots,
    left,
    right,
    new,
    res_ref,
    g_buf,
    left_buf,
    right_buf,
    new_buf,
    res_buf,
    in_sems,
    out_sems,
):
    per_dev, width, _ = res_ref.shape

    def load(slot, source, target, sem):
        return pltpu.make_async_copy(source, target, in_sems.at[slot, sem])

    def arrivals(slot):
        own = load(slot, g_ref.at[:, slot], g_buf.at[slot], 0)
        kept = [load(slot, roots[i].at[slot], new_buf[i].at[slot], 1 + i) for i in range(2)]
        first = [load(slot, left[i].at[slot], left_buf[i].at[slot], 1 + i) for i in range(2)]
        second = [load(slot, right[i].at[slot], right_buf[i].at[slot], 3 + i) for i in range(2)]
        return own, kept, first, second

    def start(copies):
        for copy in copies:
            copy.start()

    def wait(copies):
        for copy in copies:
            copy.wait()

    def begin(slot):
        own, kept, first, second = arrivals(slot)
        own.start()

        @pl.when(flag_ref[slot] == 1)
        def _():
            start(first)
            start(second)

        @pl.when(flag_ref[slot] != 1)
        def _():
            start(kept)

    begin(0)
    leaving = []
    for slot in range(per_dev):
        own, kept, first, second = arrivals(slot)
        own.wait()
        if slot + 1 < per_dev:
            begin(slot + 1)
        block = g_buf[slot].reshape(width, width)

        @pl.when(flag_ref[slot] == 1)
        def _():
            plain = lambda a: dot(a, block)
            turned = lambda a: dot_nt(a, block)
            wait(first)
            new_buf[0][slot] = finish_one(*[b[slot] for b in left_buf], plain, turned)
            wait(second)
            new_buf[1][slot] = finish_one(*[b[slot] for b in right_buf], turned, plain)

        @pl.when(flag_ref[slot] != 1)
        def _():
            wait(kept)

        outs = [
            pltpu.make_async_copy(new_buf[i].at[slot], new[i].at[slot], out_sems.at[slot, i])
            for i in range(2)
        ]
        start(outs)
        half = dot(new_buf[0][slot], block).astype(BF)
        res_buf[slot] = dot(half, new_buf[1][slot]).astype(BF)
        outs.append(
            pltpu.make_async_copy(res_buf.at[slot], res_ref.at[slot], out_sems.at[slot, 2])
        )
        outs[2].start()
        leaving += outs
    wait(leaving)


def update(flag, pieces, lroot, rroot, left, right):
    groups, per_dev, rows, width = pieces.shape
    place = pl.BlockSpec(memory_space=pl.ANY)
    shape = jax.ShapeDtypeStruct((per_dev, width, width), BF)
    half = pltpu.VMEM((per_dev, width, width), BF)
    full = pltpu.VMEM((per_dev, width, width), F32)
    pair = pltpu.VMEM((per_dev, width, 2 * width), BF)
    return pl.pallas_call(
        update_kernel,
        out_shape=((shape, shape), shape),
        in_specs=[
            pl.BlockSpec(memory_space=pltpu.SMEM),
            place,
            (place, place),
            (place,) * 2,
            (place,) * 2,
        ],
        out_specs=((place, place), place),
        scratch_shapes=[
            pltpu.VMEM((per_dev, groups, rows, width), BF),
            (pair, full),
            (pair, full),
            (half, half),
            half,
            pltpu.SemaphoreType.DMA((per_dev, 5)),
            pltpu.SemaphoreType.DMA((per_dev, 3)),
        ],
        compiler_params=pltpu.CompilerParams(vmem_limit_bytes=UPD * MIB),
        name="update",
    )(flag, pieces, (lroot, rroot), left, right)


def swap_cores(roots):
    pairs = [(source, source ^ 1) for source in range(lax.axis_size("rep"))]
    return lax.ppermute(roots, "rep", pairs)


def swap_owners(blocks, mask):
    pairs = [(source, source ^ mask) for source in range(lax.axis_size("fsdp"))]
    return lax.ppermute(blocks, "fsdp", pairs)


def swap_chips(offset, roots):
    size = lax.axis_size("rep")

    def branch(mask):
        pairs = [(source, source ^ mask) for source in range(size)]
        return lambda value: lax.ppermute(value, "rep", pairs)

    branches = [lambda value: value] + [branch(mask) for mask in range(2, size, 2)]
    return lax.switch(lax.shift_right_logical(offset, 1), branches, roots)


def exchange(pieces):
    return lax.all_to_all(pieces, "fsdp", 0, 0, tiled=True)


def per_device(
    grads, targets, left_factor, right_factor, left_root, right_root, refresh, buddy_offset
):
    groups = lax.axis_size("fsdp")
    shape = grads.shape
    per_dev, width = shape[2], shape[3]
    total = groups * per_dev
    rows = width // groups
    cut = (groups, per_dev, rows, width)
    flag = refresh[0, 0]
    flat = targets[:, 0, :].reshape(total)
    ids = jnp.arange(total, dtype=jnp.int32)
    source = jnp.sum(jnp.where(flat[None, :] == ids[:, None], ids[None, :], 0), axis=1)
    myself = lax.axis_index("fsdp")
    across = groups // 2
    table = targets[:, 0, :]
    mine = lax.dynamic_index_in_dim(table, myself, 0, keepdims=False)
    theirs = lax.dynamic_index_in_dim(table, myself ^ across, 0, keepdims=False)
    side = (mine // per_dev) ^ myself
    offset = buddy_offset[0]

    spread = exchange(cut_blocks(grads.reshape(per_dev, groups, rows, width)))
    left = prepare(flag, left_factor[0, 0], left_root[0, 0])
    sorted_pieces = pick_pieces(source, spread.reshape(total, rows, width))
    slots = jnp.arange(per_dev, dtype=jnp.int32)
    turn = jnp.full((per_dev,), lax.rem(offset, 2), jnp.int32)
    indices = (
        jnp.concatenate([((theirs // per_dev) ^ myself) % across, across + turn]),
        jnp.concatenate([theirs % per_dev, slots]),
        jnp.concatenate([jnp.minimum(side, across), across + 1 + turn]),
        jnp.concatenate([jnp.where(side < across, mine % per_dev, slots), slots]),
    )
    sorted_pieces, left, indices = lax.optimization_barrier((sorted_pieces, left, indices))
    send_which, send_slot, home_which, home_slot = indices
    owned = exchange(sorted_pieces.reshape(cut))
    right = prepare(flag, right_factor[0, 0], right_root[0, 0])
    (lnew, rnew), result = update(
        flag, owned, left_root[0, 0], right_root[0, 0], left, right
    )

    row = tuple(swap_owners(result, mask) for mask in range(1, across))
    rmoved = swap_cores(rnew)
    lfar = swap_chips(offset, lnew)
    row, rmoved, lfar = lax.optimization_barrier((row, rmoved, lfar))
    row = (result,) + row
    leaving, rnear = choose_blocks(
        send_which,
        send_slot,
        row + (rnew, rmoved),
    )
    other = swap_owners(leaving, across)
    lmoved = swap_cores(lfar)
    rcopy = swap_chips(offset, rnear)
    other, lmoved, rcopy = lax.optimization_barrier((other, lmoved, rcopy))
    precond, lcopy = choose_blocks(
        home_which,
        home_slot,
        row + (other, lfar, lmoved),
    )
    return (
        lnew.reshape(shape),
        rnew.reshape(shape),
        lcopy.reshape(shape),
        rcopy.reshape(shape),
        precond.reshape(shape),
    )


def solution(mesh):
    block = P("fsdp", "rep", None, None, None)
    placed = (
        block,
        P(None, "rep", None),
        block,
        block,
        block,
        block,
        P("fsdp", "rep", None),
        P("fsdp"),
    )
    return jax.shard_map(
        per_device,
        mesh=mesh,
        in_specs=placed,
        out_specs=(block,) * 5,
        check_vma=False,
    )
```

```python
import functools

import jax
import jax.numpy as jnp
from jax import lax
from jax.experimental import pallas as pl
from jax.experimental.pallas import tpu as pltpu
from jax.sharding import PartitionSpec as P

BF = jnp.bfloat16
F32 = jnp.float32
MIB = 2**20
PREP = 56
UPD = 56
CHOOSE = 8


def dot(a, b):
    return jnp.dot(a, b, preferred_element_type=F32)


def dot_nt(a, b):
    return lax.dot_general(a, b, (((1,), (1,)), ((), ())), preferred_element_type=F32)


def split(a):
    high = a.astype(BF)
    return high, (a - high.astype(F32)).astype(BF)


def dot3(a, b):
    return dot(a[0], b[0]) + (dot(a[0], b[1]) + dot(a[1], b[0]))


def cut_kernel(x_ref, o_ref, sems):
    copies = [
        pltpu.make_async_copy(x_ref.at[block], o_ref.at[:, block], sems.at[block])
        for block in range(x_ref.shape[0])
    ]
    for copy in copies:
        copy.start()
    for copy in copies:
        copy.wait()


def cut_blocks(blocks):
    per_dev, groups, rows, width = blocks.shape
    return pl.pallas_call(
        cut_kernel,
        out_shape=jax.ShapeDtypeStruct((groups, per_dev, rows, width), blocks.dtype),
        in_specs=[pl.BlockSpec(memory_space=pl.ANY)],
        out_specs=pl.BlockSpec(memory_space=pltpu.VMEM),
        scratch_shapes=[pltpu.SemaphoreType.DMA((per_dev,))],
        compiler_params=pltpu.CompilerParams(vmem_limit_bytes=PREP * MIB),
        name="cut_blocks",
    )(blocks)


def pick_kernel(order_ref, x_ref, o_ref, sems):
    copies = [
        pltpu.make_async_copy(x_ref.at[order_ref[slot]], o_ref.at[slot], sems.at[slot])
        for slot in range(o_ref.shape[0])
    ]
    for copy in copies:
        copy.start()
    for copy in copies:
        copy.wait()


def pick_pieces(order, pieces):
    count = order.shape[0]
    return pl.pallas_call(
        pick_kernel,
        out_shape=jax.ShapeDtypeStruct((count,) + pieces.shape[1:], pieces.dtype),
        in_specs=[
            pl.BlockSpec(memory_space=pltpu.SMEM),
            pl.BlockSpec(memory_space=pl.ANY),
        ],
        out_specs=pl.BlockSpec(memory_space=pl.ANY),
        scratch_shapes=[pltpu.SemaphoreType.DMA((count,))],
        compiler_params=pltpu.CompilerParams(vmem_limit_bytes=MIB),
        name="pick_pieces",
    )(order, pieces)


def choose_kernel(count, which_ref, slot_ref, *refs):
    arrays, outs = refs[:count], refs[count:-3]
    held, in_sems, out_sems = refs[-3:]
    per_out = outs[0].shape[0]
    total = held.shape[0]
    for block in range(total):
        for index, array in enumerate(arrays):

            @pl.when(which_ref[block] == index)
            def _():
                pltpu.make_async_copy(
                    array.at[slot_ref[block]], held.at[block], in_sems.at[block]
                ).start()

    leaving = [
        pltpu.make_async_copy(
            held.at[block],
            outs[block // per_out].at[block % per_out],
            out_sems.at[block],
        )
        for block in range(total)
    ]
    for block in range(total):
        pltpu.make_async_copy(arrays[0].at[0], held.at[block], in_sems.at[block]).wait()
        leaving[block].start()
    for copy in leaving:
        copy.wait()


def choose_blocks(which, slot, arrays):
    shape, dtype = arrays[0].shape, arrays[0].dtype
    total = which.shape[0]
    outs = total // shape[0]
    return pl.pallas_call(
        functools.partial(choose_kernel, len(arrays)),
        out_shape=(jax.ShapeDtypeStruct(shape, dtype),) * outs,
        in_specs=[pl.BlockSpec(memory_space=pltpu.SMEM)] * 2
        + [pl.BlockSpec(memory_space=pl.ANY)] * len(arrays),
        out_specs=(pl.BlockSpec(memory_space=pl.ANY),) * outs,
        scratch_shapes=[
            pltpu.VMEM((total,) + shape[1:], dtype),
            pltpu.SemaphoreType.DMA((total,)),
            pltpu.SemaphoreType.DMA((total,)),
        ],
        compiler_params=pltpu.CompilerParams(vmem_limit_bytes=CHOOSE * MIB),
        name="choose_blocks",
    )(which, slot, *arrays)


def prepare_kernel(flag_ref, f_ref, x_ref, high_ref, rest_ref):
    @pl.when(flag_ref[pl.program_id(0)] == 1)
    def _():
        root = x_ref[0]
        square = split(dot(root, root))
        fourth = split(dot3(square, square))
        fifth = split(dot(root, fourth[0]) + dot(root, fourth[1]))
        high_ref[0] = fifth[0]
        rest_ref[0] = 5.0 * root.astype(F32) - dot3(fifth, split(f_ref[0]))


def prepare(flag, factor, root):
    per_dev, width, _ = root.shape
    whole = pl.BlockSpec((1, width, width), lambda s: (s, 0, 0))
    half = jax.ShapeDtypeStruct((per_dev, width, width), BF)
    full = jax.ShapeDtypeStruct((per_dev, width, width), F32)
    return pl.pallas_call(
        prepare_kernel,
        grid=(per_dev,),
        out_shape=(half, full),
        in_specs=[pl.BlockSpec(memory_space=pltpu.SMEM)] + [whole] * 2,
        out_specs=[whole] * 2,
        compiler_params=pltpu.CompilerParams(vmem_limit_bytes=PREP * MIB),
        cost_estimate=pl.CostEstimate(
            flops=9 * 2 * per_dev * width**3,
            bytes_accessed=14 * per_dev * width**2,
            transcendentals=0,
        ),
        name="prepare",
    )(flag, factor, root)


def finish_one(fifth, rest, first, second):
    return (0.25 * (rest - second(first(fifth).astype(BF)))).astype(BF)


def update_kernel(
    flag_ref,
    g_ref,
    roots,
    left,
    right,
    new,
    res_ref,
    g_buf,
    left_buf,
    right_buf,
    new_buf,
    res_buf,
    in_sems,
    out_sems,
):
    per_dev, width, _ = res_ref.shape

    def load(slot, source, target, sem):
        return pltpu.make_async_copy(source, target, in_sems.at[slot, sem])

    def arrivals(slot):
        own = load(slot, g_ref.at[:, slot], g_buf.at[slot], 0)
        kept = [load(slot, roots[i].at[slot], new_buf[i].at[slot], 1 + i) for i in range(2)]
        first = [load(slot, left[i].at[slot], left_buf[i].at[slot], 1 + i) for i in range(2)]
        second = [load(slot, right[i].at[slot], right_buf[i].at[slot], 3 + i) for i in range(2)]
        return own, kept, first, second

    def start(copies):
        for copy in copies:
            copy.start()

    def wait(copies):
        for copy in copies:
            copy.wait()

    def begin(slot):
        own, kept, first, second = arrivals(slot)
        own.start()

        @pl.when(flag_ref[slot] == 1)
        def _():
            start(first)
            start(second)

        @pl.when(flag_ref[slot] != 1)
        def _():
            start(kept)

    begin(0)
    leaving = []
    for slot in range(per_dev):
        own, kept, first, second = arrivals(slot)
        own.wait()
        if slot + 1 < per_dev:
            begin(slot + 1)
        block = g_buf[slot].reshape(width, width)

        @pl.when(flag_ref[slot] == 1)
        def _():
            plain = lambda a: dot(a, block)
            turned = lambda a: dot_nt(a, block)
            wait(first)
            new_buf[0][slot] = finish_one(*[b[slot] for b in left_buf], plain, turned)
            wait(second)
            new_buf[1][slot] = finish_one(*[b[slot] for b in right_buf], turned, plain)

        @pl.when(flag_ref[slot] != 1)
        def _():
            wait(kept)

        outs = [
            pltpu.make_async_copy(new_buf[i].at[slot], new[i].at[slot], out_sems.at[slot, i])
            for i in range(2)
        ]
        start(outs)
        half = dot(new_buf[0][slot], block).astype(BF)
        res_buf[slot] = dot(half, new_buf[1][slot]).astype(BF)
        outs.append(
            pltpu.make_async_copy(res_buf.at[slot], res_ref.at[slot], out_sems.at[slot, 2])
        )
        outs[2].start()
        leaving += outs
    wait(leaving)


def update(flag, pieces, lroot, rroot, left, right):
    groups, per_dev, rows, width = pieces.shape
    place = pl.BlockSpec(memory_space=pl.ANY)
    shape = jax.ShapeDtypeStruct((per_dev, width, width), BF)
    half = pltpu.VMEM((per_dev, width, width), BF)
    full = pltpu.VMEM((per_dev, width, width), F32)
    return pl.pallas_call(
        update_kernel,
        out_shape=((shape, shape), shape),
        in_specs=[
            pl.BlockSpec(memory_space=pltpu.SMEM),
            place,
            (place, place),
            (place,) * 2,
            (place,) * 2,
        ],
        out_specs=((place, place), place),
        scratch_shapes=[
            pltpu.VMEM((per_dev, groups, rows, width), BF),
            (half, full),
            (half, full),
            (half, half),
            half,
            pltpu.SemaphoreType.DMA((per_dev, 5)),
            pltpu.SemaphoreType.DMA((per_dev, 3)),
        ],
        compiler_params=pltpu.CompilerParams(vmem_limit_bytes=UPD * MIB),
        name="update",
    )(flag, pieces, (lroot, rroot), left, right)


def swap_cores(roots):
    pairs = [(source, source ^ 1) for source in range(lax.axis_size("rep"))]
    return lax.ppermute(roots, "rep", pairs)


def swap_owners(blocks, mask):
    pairs = [(source, source ^ mask) for source in range(lax.axis_size("fsdp"))]
    return lax.ppermute(blocks, "fsdp", pairs)


def swap_chips(offset, roots):
    size = lax.axis_size("rep")

    def branch(mask):
        pairs = [(source, source ^ mask) for source in range(size)]
        return lambda value: lax.ppermute(value, "rep", pairs)

    branches = [lambda value: value] + [branch(mask) for mask in range(2, size, 2)]
    return lax.switch(lax.shift_right_logical(offset, 1), branches, roots)


def exchange(pieces):
    return lax.all_to_all(pieces, "fsdp", 0, 0, tiled=True)


def per_device(
    grads, targets, left_factor, right_factor, left_root, right_root, refresh, buddy_offset
):
    groups = lax.axis_size("fsdp")
    shape = grads.shape
    per_dev, width = shape[2], shape[3]
    total = groups * per_dev
    rows = width // groups
    cut = (groups, per_dev, rows, width)
    flag = refresh[0, 0]
    flat = targets[:, 0, :].reshape(total)
    ids = jnp.arange(total, dtype=jnp.int32)
    source = jnp.sum(jnp.where(flat[None, :] == ids[:, None], ids[None, :], 0), axis=1)
    myself = lax.axis_index("fsdp")
    across = groups // 2
    table = targets[:, 0, :]
    mine = lax.dynamic_index_in_dim(table, myself, 0, keepdims=False)
    theirs = lax.dynamic_index_in_dim(table, myself ^ across, 0, keepdims=False)
    side = (mine // per_dev) ^ myself
    offset = buddy_offset[0]

    spread = exchange(cut_blocks(grads.reshape(per_dev, groups, rows, width)))
    left = prepare(flag, left_factor[0, 0], left_root[0, 0])
    sorted_pieces = pick_pieces(source, spread.reshape(total, rows, width))
    slots = jnp.arange(per_dev, dtype=jnp.int32)
    turn = jnp.full((per_dev,), lax.rem(offset, 2), jnp.int32)
    indices = (
        jnp.concatenate([((theirs // per_dev) ^ myself) % across, across + turn]),
        jnp.concatenate([theirs % per_dev, slots]),
        jnp.concatenate([jnp.minimum(side, across), across + 1 + turn]),
        jnp.concatenate([jnp.where(side < across, mine % per_dev, slots), slots]),
    )
    sorted_pieces, left, indices = lax.optimization_barrier((sorted_pieces, left, indices))
    send_which, send_slot, home_which, home_slot = indices
    owned = exchange(sorted_pieces.reshape(cut))
    right = prepare(flag, right_factor[0, 0], right_root[0, 0])
    (lnew, rnew), result = update(
        flag, owned, left_root[0, 0], right_root[0, 0], left, right
    )

    row = tuple(swap_owners(result, mask) for mask in range(1, across))
    rmoved = swap_cores(rnew)
    lfar = swap_chips(offset, lnew)
    row, rmoved, lfar = lax.optimization_barrier((row, rmoved, lfar))
    row = (result,) + row
    leaving, rnear = choose_blocks(
        send_which,
        send_slot,
        row + (rnew, rmoved),
    )
    other = swap_owners(leaving, across)
    lmoved = swap_cores(lfar)
    rcopy = swap_chips(offset, rnear)
    other, lmoved, rcopy = lax.optimization_barrier((other, lmoved, rcopy))
    precond, lcopy = choose_blocks(
        home_which,
        home_slot,
        row + (other, lfar, lmoved),
    )
    return (
        lnew.reshape(shape),
        rnew.reshape(shape),
        lcopy.reshape(shape),
        rcopy.reshape(shape),
        precond.reshape(shape),
    )


def solution(mesh):
    block = P("fsdp", "rep", None, None, None)
    placed = (
        block,
        P(None, "rep", None),
        block,
        block,
        block,
        block,
        P("fsdp", "rep", None),
        P("fsdp"),
    )
    return jax.shard_map(
        per_device,
        mesh=mesh,
        in_specs=placed,
        out_specs=(block,) * 5,
        check_vma=False,
    )
```

```python
import functools

import jax
import jax.numpy as jnp
from jax import lax
from jax.experimental import pallas as pl
from jax.experimental.pallas import tpu as pltpu
from jax.sharding import PartitionSpec as P

BF = jnp.bfloat16
F32 = jnp.float32
MIB = 2**20
PREP = 56
UPD = 56
CHOOSE = 8
CHUNKS = 4


def dot(a, b):
    return jnp.dot(a, b, preferred_element_type=F32)


def dot_nt(a, b):
    return lax.dot_general(a, b, (((1,), (1,)), ((), ())), preferred_element_type=F32)


def split(a):
    high = a.astype(BF)
    return high, (a - high.astype(F32)).astype(BF)


def dot3(a, b):
    return dot(a[0], b[0]) + (dot(a[0], b[1]) + dot(a[1], b[0]))


def cut_kernel(x_ref, o_ref, sems):
    copies = [
        pltpu.make_async_copy(x_ref.at[block], o_ref.at[:, block], sems.at[block])
        for block in range(x_ref.shape[0])
    ]
    for copy in copies:
        copy.start()
    for copy in copies:
        copy.wait()


def cut_blocks(blocks):
    per_dev, groups, rows, width = blocks.shape
    return pl.pallas_call(
        cut_kernel,
        out_shape=jax.ShapeDtypeStruct((groups, per_dev, rows, width), blocks.dtype),
        in_specs=[pl.BlockSpec(memory_space=pl.ANY)],
        out_specs=pl.BlockSpec(memory_space=pltpu.VMEM),
        scratch_shapes=[pltpu.SemaphoreType.DMA((per_dev,))],
        compiler_params=pltpu.CompilerParams(vmem_limit_bytes=PREP * MIB),
        name="cut_blocks",
    )(blocks)


def pick_kernel(order_ref, x_ref, o_ref, sems):
    copies = [
        pltpu.make_async_copy(x_ref.at[order_ref[slot]], o_ref.at[slot], sems.at[slot])
        for slot in range(o_ref.shape[0])
    ]
    for copy in copies:
        copy.start()
    for copy in copies:
        copy.wait()


def pick_pieces(order, pieces):
    count = order.shape[0]
    return pl.pallas_call(
        pick_kernel,
        out_shape=jax.ShapeDtypeStruct((count,) + pieces.shape[1:], pieces.dtype),
        in_specs=[
            pl.BlockSpec(memory_space=pltpu.SMEM),
            pl.BlockSpec(memory_space=pl.ANY),
        ],
        out_specs=pl.BlockSpec(memory_space=pl.ANY),
        scratch_shapes=[pltpu.SemaphoreType.DMA((count,))],
        compiler_params=pltpu.CompilerParams(vmem_limit_bytes=MIB),
        name="pick_pieces",
    )(order, pieces)


def choose_kernel(count, which_ref, slot_ref, *refs):
    arrays, outs = refs[:count], refs[count:-3]
    held, in_sems, out_sems = refs[-3:]
    per_out = outs[0].shape[0]
    total = held.shape[0]
    rows = held.shape[1] // CHUNKS
    parts = [(block, part) for block in range(total) for part in range(CHUNKS)]

    def come(array, slot, block, part):
        span = pl.ds(part * rows, rows)
        return pltpu.make_async_copy(
            array.at[slot, span], held.at[block, span], in_sems.at[block, part]
        )

    def leave(block, part):
        span = pl.ds(part * rows, rows)
        return pltpu.make_async_copy(
            held.at[block, span],
            outs[block // per_out].at[block % per_out, span],
            out_sems.at[block, part],
        )

    for block in range(total):
        for index, array in enumerate(arrays):

            @pl.when(which_ref[block] == index)
            def _():
                for part in range(CHUNKS):
                    come(array, slot_ref[block], block, part).start()

    for block, part in parts:
        come(arrays[0], 0, block, part).wait()
        leave(block, part).start()
    for block, part in parts:
        leave(block, part).wait()


def choose_blocks(which, slot, arrays):
    shape, dtype = arrays[0].shape, arrays[0].dtype
    total = which.shape[0]
    outs = total // shape[0]
    return pl.pallas_call(
        functools.partial(choose_kernel, len(arrays)),
        out_shape=(jax.ShapeDtypeStruct(shape, dtype),) * outs,
        in_specs=[pl.BlockSpec(memory_space=pltpu.SMEM)] * 2
        + [pl.BlockSpec(memory_space=pl.ANY)] * len(arrays),
        out_specs=(pl.BlockSpec(memory_space=pl.ANY),) * outs,
        scratch_shapes=[
            pltpu.VMEM((total,) + shape[1:], dtype),
            pltpu.SemaphoreType.DMA((total, CHUNKS)),
            pltpu.SemaphoreType.DMA((total, CHUNKS)),
        ],
        compiler_params=pltpu.CompilerParams(vmem_limit_bytes=CHOOSE * MIB),
        name="choose_blocks",
    )(which, slot, *arrays)


def prepare_kernel(flag_ref, f_ref, x_ref, high_ref, rest_ref):
    @pl.when(flag_ref[pl.program_id(0)] == 1)
    def _():
        root = x_ref[0]
        square = split(dot(root, root))
        fourth = split(dot3(square, square))
        fifth = split(dot(root, fourth[0]) + dot(root, fourth[1]))
        high_ref[0] = fifth[0]
        rest_ref[0] = 5.0 * root.astype(F32) - dot3(fifth, split(f_ref[0]))


def prepare(flag, factor, root):
    per_dev, width, _ = root.shape
    whole = pl.BlockSpec((1, width, width), lambda s: (s, 0, 0))
    half = jax.ShapeDtypeStruct((per_dev, width, width), BF)
    full = jax.ShapeDtypeStruct((per_dev, width, width), F32)
    return pl.pallas_call(
        prepare_kernel,
        grid=(per_dev,),
        out_shape=(half, full),
        in_specs=[pl.BlockSpec(memory_space=pltpu.SMEM)] + [whole] * 2,
        out_specs=[whole] * 2,
        compiler_params=pltpu.CompilerParams(vmem_limit_bytes=PREP * MIB),
        cost_estimate=pl.CostEstimate(
            flops=9 * 2 * per_dev * width**3,
            bytes_accessed=14 * per_dev * width**2,
            transcendentals=0,
        ),
        name="prepare",
    )(flag, factor, root)


def finish_one(fifth, rest, first, second):
    return (0.25 * (rest - second(first(fifth).astype(BF)))).astype(BF)


def update_kernel(
    flag_ref,
    g_ref,
    roots,
    left,
    right,
    new,
    res_ref,
    g_buf,
    left_buf,
    right_buf,
    new_buf,
    res_buf,
    in_sems,
    out_sems,
):
    per_dev, width, _ = res_ref.shape

    def load(slot, source, target, sem):
        return pltpu.make_async_copy(source, target, in_sems.at[slot, sem])

    def arrivals(slot):
        own = load(slot, g_ref.at[:, slot], g_buf.at[slot], 0)
        kept = [load(slot, roots[i].at[slot], new_buf[i].at[slot], 1 + i) for i in range(2)]
        first = [load(slot, left[i].at[slot], left_buf[i].at[slot], 1 + i) for i in range(2)]
        second = [load(slot, right[i].at[slot], right_buf[i].at[slot], 3 + i) for i in range(2)]
        return own, kept, first, second

    def start(copies):
        for copy in copies:
            copy.start()

    def wait(copies):
        for copy in copies:
            copy.wait()

    def begin(slot):
        own, kept, first, second = arrivals(slot)
        own.start()

        @pl.when(flag_ref[slot] == 1)
        def _():
            start(first)
            start(second)

        @pl.when(flag_ref[slot] != 1)
        def _():
            start(kept)

    begin(0)
    leaving = []
    for slot in range(per_dev):
        own, kept, first, second = arrivals(slot)
        own.wait()
        if slot + 1 < per_dev:
            begin(slot + 1)
        block = g_buf[slot].reshape(width, width)

        @pl.when(flag_ref[slot] == 1)
        def _():
            plain = lambda a: dot(a, block)
            turned = lambda a: dot_nt(a, block)
            wait(first)
            new_buf[0][slot] = finish_one(*[b[slot] for b in left_buf], plain, turned)
            wait(second)
            new_buf[1][slot] = finish_one(*[b[slot] for b in right_buf], turned, plain)

        @pl.when(flag_ref[slot] != 1)
        def _():
            wait(kept)

        outs = [
            pltpu.make_async_copy(new_buf[i].at[slot], new[i].at[slot], out_sems.at[slot, i])
            for i in range(2)
        ]
        start(outs)
        half = dot(new_buf[0][slot], block).astype(BF)
        res_buf[slot] = dot(half, new_buf[1][slot]).astype(BF)
        outs.append(
            pltpu.make_async_copy(res_buf.at[slot], res_ref.at[slot], out_sems.at[slot, 2])
        )
        outs[2].start()
        leaving += outs
    wait(leaving)


def update(flag, pieces, lroot, rroot, left, right):
    groups, per_dev, rows, width = pieces.shape
    place = pl.BlockSpec(memory_space=pl.ANY)
    shape = jax.ShapeDtypeStruct((per_dev, width, width), BF)
    half = pltpu.VMEM((per_dev, width, width), BF)
    full = pltpu.VMEM((per_dev, width, width), F32)
    return pl.pallas_call(
        update_kernel,
        out_shape=((shape, shape), shape),
        in_specs=[
            pl.BlockSpec(memory_space=pltpu.SMEM),
            place,
            (place, place),
            (place,) * 2,
            (place,) * 2,
        ],
        out_specs=((place, place), place),
        scratch_shapes=[
            pltpu.VMEM((per_dev, groups, rows, width), BF),
            (half, full),
            (half, full),
            (half, half),
            half,
            pltpu.SemaphoreType.DMA((per_dev, 5)),
            pltpu.SemaphoreType.DMA((per_dev, 3)),
        ],
        compiler_params=pltpu.CompilerParams(vmem_limit_bytes=UPD * MIB),
        name="update",
    )(flag, pieces, (lroot, rroot), left, right)


def swap_cores(roots):
    pairs = [(source, source ^ 1) for source in range(lax.axis_size("rep"))]
    return lax.ppermute(roots, "rep", pairs)


def swap_owners(blocks, mask):
    pairs = [(source, source ^ mask) for source in range(lax.axis_size("fsdp"))]
    return lax.ppermute(blocks, "fsdp", pairs)


def swap_chips(offset, roots):
    size = lax.axis_size("rep")

    def branch(mask):
        pairs = [(source, source ^ mask) for source in range(size)]
        return lambda value: lax.ppermute(value, "rep", pairs)

    branches = [lambda value: value] + [branch(mask) for mask in range(2, size, 2)]
    return lax.switch(lax.shift_right_logical(offset, 1), branches, roots)


def exchange(pieces):
    return lax.all_to_all(pieces, "fsdp", 0, 0, tiled=True)


def per_device(
    grads, targets, left_factor, right_factor, left_root, right_root, refresh, buddy_offset
):
    groups = lax.axis_size("fsdp")
    shape = grads.shape
    per_dev, width = shape[2], shape[3]
    total = groups * per_dev
    rows = width // groups
    cut = (groups, per_dev, rows, width)
    flag = refresh[0, 0]
    flat = targets[:, 0, :].reshape(total)
    ids = jnp.arange(total, dtype=jnp.int32)
    source = jnp.sum(jnp.where(flat[None, :] == ids[:, None], ids[None, :], 0), axis=1)
    myself = lax.axis_index("fsdp")
    across = groups // 2
    table = targets[:, 0, :]
    mine = lax.dynamic_index_in_dim(table, myself, 0, keepdims=False)
    theirs = lax.dynamic_index_in_dim(table, myself ^ across, 0, keepdims=False)
    side = (mine // per_dev) ^ myself
    offset = buddy_offset[0]

    spread = exchange(cut_blocks(grads.reshape(per_dev, groups, rows, width)))
    left = prepare(flag, left_factor[0, 0], left_root[0, 0])
    sorted_pieces = pick_pieces(source, spread.reshape(total, rows, width))
    slots = jnp.arange(per_dev, dtype=jnp.int32)
    turn = jnp.full((per_dev,), lax.rem(offset, 2), jnp.int32)
    indices = (
        jnp.concatenate([((theirs // per_dev) ^ myself) % across, across + turn]),
        jnp.concatenate([theirs % per_dev, slots]),
        jnp.concatenate([jnp.minimum(side, across), across + 1 + turn]),
        jnp.concatenate([jnp.where(side < across, mine % per_dev, slots), slots]),
    )
    sorted_pieces, left, indices = lax.optimization_barrier((sorted_pieces, left, indices))
    send_which, send_slot, home_which, home_slot = indices
    owned = exchange(sorted_pieces.reshape(cut))
    right = prepare(flag, right_factor[0, 0], right_root[0, 0])
    (lnew, rnew), result = update(
        flag, owned, left_root[0, 0], right_root[0, 0], left, right
    )

    row = tuple(swap_owners(result, mask) for mask in range(1, across))
    rmoved = swap_cores(rnew)
    lfar = swap_chips(offset, lnew)
    row, rmoved, lfar = lax.optimization_barrier((row, rmoved, lfar))
    row = (result,) + row
    leaving, rnear = choose_blocks(
        send_which,
        send_slot,
        row + (rnew, rmoved),
    )
    other = swap_owners(leaving, across)
    lmoved = swap_cores(lfar)
    rcopy = swap_chips(offset, rnear)
    other, lmoved, rcopy = lax.optimization_barrier((other, lmoved, rcopy))
    precond, lcopy = choose_blocks(
        home_which,
        home_slot,
        row + (other, lfar, lmoved),
    )
    return (
        lnew.reshape(shape),
        rnew.reshape(shape),
        lcopy.reshape(shape),
        rcopy.reshape(shape),
        precond.reshape(shape),
    )


def solution(mesh):
    block = P("fsdp", "rep", None, None, None)
    placed = (
        block,
        P(None, "rep", None),
        block,
        block,
        block,
        block,
        P("fsdp", "rep", None),
        P("fsdp"),
    )
    return jax.shard_map(
        per_device,
        mesh=mesh,
        in_specs=placed,
        out_specs=(block,) * 5,
        check_vma=False,
    )
```
